32 devices in a mesh: groups: 2 (over y), inst: 4 (over z), tp: 4 (over x, core).
Axes of the slice: x: 2, y: 2, z: 4, core: 2. Of those that a mesh axis runs over, the one named last changes fastest.
Arguments:
- tokens: bfloat16 [4, 2048, 8192], P(None, ('groups', 'inst'), 'tp'), parts along dimension 1, may hold values from -6 to 6
- key_value_weight: bfloat16 [8192, 2048], P('tp'), may hold values from -0.0625 to 0.0625
- adapter_down_weight: bfloat16 [64, 8192, 256], P(('groups', 'inst'), 'tp'), parts along dimension 0, may hold values from -0.0625 to 0.0625
- adapter_up_weight: bfloat16 [64, 2, 128, 1024], P(('groups', 'inst'), None, None, 'tp'), parts along dimension 0, may hold values from -0.5 to 0.5
- row_adapter_index: int32 [4, 2048], P(None, ('groups', 'inst')), parts along dimension 1, may hold values from 0 to 31, as said below
- ranks: int32 [64], P(('groups', 'inst')), parts along dimension 0, may hold values from 16 to 128, as said below
Outputs:
- kv_out: bfloat16 [4, 2048, 2, 1024], P(None, ('groups', 'inst'), None, 'tp'), parts along dimension 1
The draws below stay inside these ranges and needn't reach their ends.
There are 2 independent parts, one for each index of `groups`. The reference program is written for one: setup_inputs(seed, part) draws one part's arguments, and reference() takes and returns one part's arrays. A program takes and returns all parts, laid end to end along the dimension named above; an argument that names none is the same for every part. Nothing has to cross between parts.
Inputs may be any that keep to these rules, and one draw needn't show every extreme that they name: `row_adapter_index`: adapter a is held by instance a // 8. In each step the 256 rows of one instance name adapters of one holder at most 128 times, and of some holder exactly 128 times. `ranks`: multiples of 16.
All inputs are finite; a program needn't handle non-finite values.
Results may differ from the reference program's by a relative error of at most 0.014.
Values may be sent and summed in bfloat16 or wider, within the bound.
No kernel may reach another device: no remote copies, remote signals or barrier semaphores. Data moves between devices by JAX's collectives and lax.ppermute only.
A program may use at most 128 MiB of HBM per device.

```python
import jax
import jax.numpy as jnp
from jax import lax

MODEL_WIDTH = 8192
KEY_VALUE_WIDTH = 1024
PADDED_RANK = 128
STEPS = 4
ROWS_INST = 256
ADP_DEV = 8
GROUP_ADAPTERS = 32
ROWS = 1024
CAPACITY = 128
N_TP = 4


def draw_row_adapter_index(key, part):
    key = jax.random.fold_in(key, 11)
    holders = GROUP_ADAPTERS // ADP_DEV

    def one_block(block_key):
        first_key, other_key, order_key, within_key = jax.random.split(block_key, 4)
        first = jax.random.randint(first_key, (), 0, holders)
        others = jax.random.permutation(other_key, (holders - 1) * CAPACITY)[:ROWS_INST - CAPACITY]
        other_holder = others // CAPACITY
        other_holder = other_holder + (other_holder >= first).astype(jnp.int32)
        slot_holder = jnp.concatenate([jnp.full((CAPACITY,), first, jnp.int32), other_holder.astype(jnp.int32)])
        order = jax.random.permutation(order_key, ROWS_INST)
        holder = slot_holder[order]
        within = jax.random.randint(within_key, (ROWS_INST,), 0, ADP_DEV)
        return (holder * ADP_DEV + within).astype(jnp.int32)
    keys = jax.random.split(key, STEPS * holders)
    return jax.vmap(one_block)(keys).reshape(STEPS, holders * ROWS_INST)


def draw_ranks(key, part):
    key = jax.random.fold_in(key, 12)
    first_key, second_key = jax.random.split(key)
    values = PADDED_RANK // 8 * jax.random.randint(first_key, (GROUP_ADAPTERS,), 1, 9)
    chosen = jax.random.randint(second_key, (), 0, GROUP_ADAPTERS)
    return jnp.where(jnp.arange(GROUP_ADAPTERS) == chosen, PADDED_RANK, values).astype(jnp.int32)


def block_levels(stream_key, dims, cuts, low, largest):
    def one(position, blocks):
        draws = jax.random.uniform(jax.random.fold_in(jax.random.fold_in(stream_key, 6), position), (blocks,), jnp.float32, low / len(cuts), largest / len(cuts))
        return jnp.repeat(jnp.exp(draws), dims[position] // blocks).reshape((-1,) + (1,) * (len(dims) - position - 1))

    loudness = one(*cuts[0])
    for cut in cuts[1:]:
        loudness = loudness * one(*cut)
    return loudness


def noise(rng, extent, scale, limit, cuts=(), dtype=jnp.bfloat16):
    array = jax.random.normal(rng, extent, jnp.float32) * scale
    if len(cuts) > 0:
        array = block_levels(rng, extent, cuts, -0.22, 0.18) * array
    return jnp.clip(array, min=-limit, max=limit).astype(dtype)


def setup_inputs(seed: int = 0, part: int = 0) -> dict:
    splits = jax.random.split(jax.random.key(seed), 7)
    part_splits = jax.random.split(jax.random.fold_in(splits[6], part), 7)
    return {
        "tokens": noise(part_splits[0], (STEPS, ROWS, MODEL_WIDTH), 1.0, 6.0, ((1, 4), (2, 4))),
        "key_value_weight": noise(splits[1], (MODEL_WIDTH, 2 * KEY_VALUE_WIDTH), MODEL_WIDTH ** -0.5, 0.0625, ((0, 4),)),
        "adapter_down_weight": noise(part_splits[2], (GROUP_ADAPTERS, MODEL_WIDTH, 2 * PADDED_RANK), MODEL_WIDTH ** -0.5, 0.0625, ((0, 4), (1, 4))),
        "adapter_up_weight": noise(part_splits[3], (GROUP_ADAPTERS, 2, PADDED_RANK, KEY_VALUE_WIDTH), PADDED_RANK ** -0.5, 0.5, ((0, 4), (3, 4))),
        "row_adapter_index": draw_row_adapter_index(jax.random.fold_in(jax.random.fold_in(splits[6], part), 71), part),
        "ranks": draw_ranks(jax.random.fold_in(jax.random.fold_in(splits[6], part), 71), part),
    }


def reference(tokens, key_value_weight, adapter_down_weight, adapter_up_weight, row_adapter_index, ranks):
    width = MODEL_WIDTH // N_TP
    weight_parts = key_value_weight.reshape(N_TP, width, 2 * KEY_VALUE_WIDTH).astype(jnp.float32)

    def row_block(block_args):
        rows_x, row_index_list = block_args
        down_matrices = adapter_down_weight[row_index_list].astype(jnp.float32)
        shrunk_rows = jnp.einsum('nd,ndr->nr', rows_x.astype(jnp.float32), down_matrices)
        rank_rows = ranks[row_index_list]
        keep = (jnp.arange(2 * PADDED_RANK)[None, :] % PADDED_RANK) < rank_rows[:, None]
        shrunk_rows = jnp.where(keep, shrunk_rows, 0.0).astype(jnp.bfloat16)
        up_matrices = adapter_up_weight[row_index_list].astype(jnp.float32)
        delta = jnp.einsum('nkr,nkrc->nkc', shrunk_rows.reshape(-1, 2, PADDED_RANK).astype(jnp.float32), up_matrices)
        return delta.astype(jnp.bfloat16)

    def one_step(step_args):
        x_step, ids_step = step_args
        x_parts = x_step.reshape(ROWS, N_TP, width).astype(jnp.float32)
        partial_value = jnp.einsum('ntd,tdc->tnc', x_parts, weight_parts).astype(jnp.bfloat16)
        partial_value = lax.optimization_barrier(partial_value)
        base = jnp.sum(partial_value.astype(jnp.float32), axis=0).reshape(ROWS, 2, KEY_VALUE_WIDTH)
        delta = lax.map(row_block, (x_step.reshape(-1, 16, MODEL_WIDTH), ids_step.reshape(-1, 16)))
        delta = delta.reshape(ROWS, 2, KEY_VALUE_WIDTH)
        return (base + delta.astype(jnp.float32)).astype(jnp.bfloat16)

    return lax.map(one_step, (tokens, row_adapter_index))
```

```python
import jax
import jax.numpy as jnp
from jax import lax
from jax.experimental import pallas as pl
from jax.experimental.pallas import tpu as pltpu
from jax.sharding import PartitionSpec as P

VMEM = 48 * 1024 * 1024


def down_kernel(ranks_ref, ids_ref, x_ref, weight_ref, out_ref, acc_ref):
    adapter = pl.program_id(0)

    @pl.when(adapter == 0)
    def _():
        acc_ref[...] = jnp.zeros_like(acc_ref)

    part = jnp.dot(x_ref[...], weight_ref[0], preferred_element_type=jnp.float32)
    column = lax.broadcasted_iota(jnp.int32, part.shape, 1) % (part.shape[1] // 2)
    keep = (ids_ref[...] == adapter) & (column < ranks_ref[adapter])
    acc_ref[...] += jnp.where(keep, part, 0.0)

    @pl.when(adapter == pl.num_programs(0) - 1)
    def _():
        out_ref[...] = acc_ref[...].astype(out_ref.dtype)


def down(x, ids, weight, ranks):
    rows, width = x.shape
    adapters, _, rank2 = weight.shape
    return pl.pallas_call(
        down_kernel,
        out_shape=jax.ShapeDtypeStruct((rows, rank2), jnp.bfloat16),
        grid=(adapters,),
        in_specs=[
            pl.BlockSpec(memory_space=pltpu.SMEM),
            pl.BlockSpec((rows, 1), lambda a: (0, 0)),
            pl.BlockSpec((rows, width), lambda a: (0, 0)),
            pl.BlockSpec((1, width, rank2), lambda a: (a, 0, 0)),
        ],
        out_specs=pl.BlockSpec((rows, rank2), lambda a: (0, 0)),
        scratch_shapes=[pltpu.VMEM((rows, rank2), jnp.float32)],
        compiler_params=pltpu.CompilerParams(vmem_limit_bytes=VMEM),
        cost_estimate=pl.CostEstimate(
            flops=2 * rows * width * adapters * rank2,
            bytes_accessed=2 * (rows * width + adapters * width * rank2 + rows * rank2),
            transcendentals=0,
        ),
        name="down",
    )(ranks, ids, x, weight)


def up_kernel(count, *refs):
    ids_ref, parts, weight_ref, out_ref = refs[0], refs[1 : 1 + count], refs[-2], refs[-1]
    adapters, halves, rank, columns = weight_ref.shape
    total = parts[0][...].astype(jnp.float32)
    for part in parts[1:]:
        total = total + part[...].astype(jnp.float32)
    ids = ids_ref[...]
    for half in range(halves):
        mine = total[:, half * rank : (half + 1) * rank]
        spread = jnp.concatenate(
            [jnp.where(ids == a, mine, 0.0).astype(jnp.bfloat16) for a in range(adapters)], axis=1
        )
        matrix = weight_ref[:, half].reshape(adapters * rank, columns)
        out_ref[:, half * columns : (half + 1) * columns] = jnp.dot(
            spread, matrix, preferred_element_type=jnp.float32
        ).astype(out_ref.dtype)


def up(parts, ids, weight):
    rows = ids.shape[0]
    adapters, halves, rank, columns = weight.shape
    whole = pl.BlockSpec(memory_space=pltpu.VMEM)
    return pl.pallas_call(
        lambda *refs: up_kernel(len(parts), *refs),
        out_shape=jax.ShapeDtypeStruct((rows, halves * columns), jnp.bfloat16),
        in_specs=[whole] * (2 + len(parts)),
        out_specs=whole,
        compiler_params=pltpu.CompilerParams(vmem_limit_bytes=VMEM),
        cost_estimate=pl.CostEstimate(
            flops=2 * rows * adapters * halves * rank * columns,
            bytes_accessed=2 * (weight.size + rows * halves * (columns + rank * len(parts))),
            transcendentals=0,
        ),
        name="up",
    )(ids, *parts, weight)


def swap(x, axis, distance):
    count = lax.axis_size(axis)
    return lax.ppermute(x, axis, [(i, i ^ distance) for i in range(count)])


def after(x, *others):
    return lax.optimization_barrier((x, *others))[0]


def local(tokens, key_value_weight, adapter_down_weight, adapter_up_weight, row_adapter_index, ranks):
    steps, step_rows, width = tokens.shape
    inst_count = lax.axis_size("inst")
    tp_count = lax.axis_size("tp")
    held, _, rank2 = adapter_down_weight.shape
    halves, columns = adapter_up_weight.shape[1], adapter_up_weight.shape[3]
    rows = steps * step_rows
    me = lax.axis_index("inst")
    tp_me = lax.axis_index("tp")
    x = tokens.reshape(rows, width)
    ids = row_adapter_index.reshape(1, rows)
    chunk = 128
    pooled = inst_count == 4
    if pooled:
        own_cap, near_cap, far_cap, flex_cap = rows // 2, 448 * rows // 1024, rows // 4, 192 * rows // 1024
    else:
        own_cap = near_cap = far_cap = flex_cap = 0
    holder = ids // held
    base_own, base_near = 0, own_cap
    base_far2 = base_near + near_cap
    base_far3 = base_far2 + far_cap
    base_flex = base_far3 + far_cap
    base_over = base_flex + flex_cap
    if pooled:
        cls = holder ^ me
        hit = (cls == jnp.arange(4)[:, None]).astype(jnp.bfloat16)
        earlier = (jnp.arange(rows)[:, None] < jnp.arange(rows)[None, :]).astype(jnp.bfloat16)
        before = jnp.dot(hit, earlier, preferred_element_type=jnp.float32).astype(jnp.int32)
        counts = jnp.sum(hit.astype(jnp.int32), axis=1)
        place = jnp.sum(jnp.where(hit > 0, before, 0), axis=0, keepdims=True)
        over_near = jnp.maximum(counts[1] - near_cap, 0)
        extra2 = jnp.maximum(counts[2] - far_cap, 0)
        extra3 = jnp.maximum(counts[3] - far_cap, 0)
        over_far = jnp.maximum(extra2 + extra3 - flex_cap, 0)
        flex = place - far_cap + jnp.where(cls == 3, extra2, 0)
        far_target = jnp.where(
            place < far_cap,
            place + jnp.where(cls == 2, base_far2, base_far3),
            jnp.where(flex < flex_cap, flex + base_flex, flex - flex_cap + over_near + base_over),
        )
        near_target = jnp.where(
            place < near_cap, place + base_near, place - near_cap + base_over
        )
        target = jnp.where(cls == 0, place, jnp.where(cls == 1, near_target, far_target))
        over = over_near + over_far
    else:
        target = jnp.arange(rows)[None, :]
        over = jnp.int32(rows)

    def pick(start, size):
        sel = (start + jnp.arange(size))[:, None] == target
        slot_ids = jnp.sum(jnp.where(sel, ids + 1, 0), axis=1, keepdims=True) - 1
        return sel.astype(jnp.bfloat16), slot_ids

    def gather(sel):
        return jnp.dot(sel, x, preferred_element_type=jnp.float32).astype(jnp.bfloat16)

    def put(sel, rows_back):
        return lax.dot_general(
            sel, rows_back, (((0,), (0,)), ((), ())), preferred_element_type=jnp.float32
        )

    def held_ids(global_ids):
        local_ids = global_ids - me * held
        return jnp.where((local_ids >= 0) & (local_ids < held), local_ids, -1)

    def correction(x_list, list_ids):
        part = down(x_list, list_ids, adapter_down_weight, ranks)
        parts = [part] + [swap(part, "tp", d) for d in range(1, tp_count)]
        return up(parts, list_ids, adapter_up_weight)

    def base_parts():
        matrix = key_value_weight.reshape(width, halves, tp_count, columns)
        out = []
        for d in range(tp_count):
            block = lax.dynamic_index_in_dim(matrix, tp_me ^ d, 2, keepdims=False)
            part = jnp.dot(
                x, block.reshape(width, halves * columns), preferred_element_type=jnp.float32
            ).astype(jnp.bfloat16)
            out.append(swap(part, "tp", d) if d else part)
        total = out[0].astype(jnp.float32)
        for part in out[1:]:
            total = total + part.astype(jnp.float32)
        return total

    if pooled:
        half = far_cap // 2
        sel_flex, ids_flex = pick(base_flex, flex_cap)
        sel_far = {}
        far_ids = {}
        for d, start in ((2, base_far2), (3, base_far3)):
            sel_far[d], far_ids[d] = pick(start, far_cap)
        sel_near, ids_near = pick(base_near, near_cap)
        sel_own, ids_own = pick(base_own, own_cap)

        got2 = swap(jnp.concatenate([ids_flex, far_ids[2]], axis=0), "inst", 2)
        got3 = swap(jnp.concatenate([ids_flex, far_ids[3]], axis=0), "inst", 3)
        got1 = swap(ids_near, "inst", 1)
        got2, got3, got1 = held_ids(got2), held_ids(got3), held_ids(got1)

        x_flex = swap(gather(sel_flex), "inst", 2)
        x_near = swap(gather(sel_near), "inst", 1)
        x_2a = swap(gather(sel_far[2][:half]), "inst", 2)
        x_3a = swap(gather(after(sel_far[3][:half], x_flex)), "inst", 3)
        x_flex_on = swap(x_flex, "inst", 1)
        x_2b = swap(gather(after(sel_far[2][half:], x_2a)), "inst", 2)
        x_3b = swap(gather(after(sel_far[3][half:], x_3a)), "inst", 3)

        total = base_parts()
        total = total + put(sel_own, correction(gather(sel_own), held_ids(ids_own)))
        flex_mine = correction(x_flex, got2[:flex_cap])
        flex_other = swap(correction(x_flex_on, got3[:flex_cap]), "inst", 1)
        total = total + put(sel_near, swap(correction(x_near, got1), "inst", 1))
        total = total + put(
            sel_far[2][:half], swap(correction(x_2a, got2[flex_cap : flex_cap + half]), "inst", 2)
        )
        total = total + put(sel_flex, swap(flex_mine + flex_other, "inst", 2))
        total = total + put(
            sel_far[3][:half], swap(correction(x_3a, got3[flex_cap : flex_cap + half]), "inst", 3)
        )
        total = total + put(
            sel_far[2][half:], swap(correction(x_2b, got2[flex_cap + half :]), "inst", 2)
        )
        total = total + put(
            sel_far[3][half:], swap(correction(x_3b, got3[flex_cap + half :]), "inst", 3)
        )
    else:
        total = base_parts()

    trips = (lax.pmax(over, ("groups", "inst", "tp")) + chunk - 1) // chunk

    def more(carry):
        return carry[0] < trips

    def overflow(carry):
        trip, total = carry
        sel, slot_ids = pick(base_over + trip * chunk, chunk)
        x_all = lax.all_gather(gather(sel), "inst", axis=0, tiled=True)
        ids_all = held_ids(lax.all_gather(slot_ids, "inst", axis=0, tiled=True))
        delta = correction(x_all, ids_all)
        back = lax.all_to_all(
            delta.reshape(inst_count, chunk, halves * columns), "inst", 0, 0, tiled=True
        )
        mine = jnp.sum(back.astype(jnp.float32), axis=0).astype(jnp.bfloat16)
        return trip + 1, total + put(sel, mine)

    _, total = lax.while_loop(more, overflow, (jnp.int32(0), total))
    return total.astype(jnp.bfloat16).reshape(steps, step_rows, halves, columns)


def solution(mesh):
    placed = (
        P(None, ("groups", "inst"), "tp"),
        P("tp", None),
        P(("groups", "inst"), "tp", None),
        P(("groups", "inst"), None, None, "tp"),
        P(None, ("groups", "inst")),
        P(("groups", "inst")),
    )
    return jax.shard_map(
        local,
        mesh=mesh,
        in_specs=placed,
        out_specs=P(None, ("groups", "inst"), None, "tp"),
        check_vma=False,
    )
```

```python
import jax
import jax.numpy as jnp
from jax import lax
from jax.experimental import pallas as pl
from jax.experimental.pallas import tpu as pltpu
from jax.sharding import PartitionSpec as P

VMEM = 48 * 1024 * 1024
SMALL = pl.CostEstimate(flops=1024, bytes_accessed=1024, transcendentals=0)


def gather_kernel(starts, target_ref, x_ref, *outs):
    target = target_ref[...]
    for start, out in zip(starts, outs):
        slot = start + lax.broadcasted_iota(jnp.int32, (out.shape[0], 1), 0)
        sel = jnp.where(slot == target, 1.0, 0.0).astype(jnp.bfloat16)
        out[...] = jnp.dot(sel, x_ref[...], preferred_element_type=jnp.float32).astype(out.dtype)


def gather(starts, sizes, target, x):
    rows, width = x.shape
    tile = min(512, width)
    return pl.pallas_call(
        lambda *refs: gather_kernel(starts, *refs),
        out_shape=[jax.ShapeDtypeStruct((n, width), x.dtype) for n in sizes],
        grid=(width // tile,),
        in_specs=[
            pl.BlockSpec((1, rows), lambda c: (0, 0)),
            pl.BlockSpec((rows, tile), lambda c: (0, c)),
        ],
        out_specs=[pl.BlockSpec((n, tile), lambda c: (0, c)) for n in sizes],
        compiler_params=pltpu.CompilerParams(vmem_limit_bytes=VMEM),
        cost_estimate=SMALL,
        name="gather",
    )(target, x)


def down_kernel(count, ranks_ref, *refs):
    ids, xs = refs[:count], refs[count : 2 * count]
    weight_ref = refs[2 * count]
    outs, totals = refs[2 * count + 1 : 3 * count + 1], refs[3 * count + 1 :]
    adapter = pl.program_id(0)

    @pl.when(adapter == 0)
    def _():
        for total in totals:
            total[...] = jnp.zeros_like(total)

    for id_ref, x_ref, total in zip(ids, xs, totals):
        part = jnp.dot(x_ref[...], weight_ref[0], preferred_element_type=jnp.float32)
        column = lax.broadcasted_iota(jnp.int32, part.shape, 1) % (part.shape[1] // 2)
        keep = (id_ref[...] == adapter) & (column < ranks_ref[adapter])
        total[...] += jnp.where(keep, part, 0.0)

    @pl.when(adapter == pl.num_programs(0) - 1)
    def _():
        for total, out in zip(totals, outs):
            out[...] = total[...].astype(out.dtype)


def down(xs, ids, weight, ranks):
    count = len(xs)
    adapters, width, rank2 = weight.shape
    sizes = [x.shape[0] for x in xs]
    fixed = lambda a: (0, 0)
    return pl.pallas_call(
        lambda *refs: down_kernel(count, *refs),
        out_shape=[jax.ShapeDtypeStruct((n, rank2), jnp.bfloat16) for n in sizes],
        grid=(adapters,),
        in_specs=[pl.BlockSpec(memory_space=pltpu.SMEM)]
        + [pl.BlockSpec((n, 1), fixed) for n in sizes]
        + [pl.BlockSpec((n, width), fixed) for n in sizes]
        + [pl.BlockSpec((1, width, rank2), lambda a: (a, 0, 0))],
        out_specs=[pl.BlockSpec((n, rank2), fixed) for n in sizes],
        scratch_shapes=[pltpu.VMEM((n, rank2), jnp.float32) for n in sizes],
        compiler_params=pltpu.CompilerParams(vmem_limit_bytes=VMEM),
        cost_estimate=SMALL,
        name="down",
    )(ranks, *ids, *xs, weight)


def up_kernel(count, *refs):
    ids, parts, weight_ref, outs = refs[:count], refs[count : 2 * count], refs[2 * count], refs[-count:]
    adapters, halves, rank, columns = weight_ref.shape
    for id_ref, part_ref, out in zip(ids, parts, outs):
        total = part_ref[0].astype(jnp.float32)
        for n in range(1, part_ref.shape[0]):
            total = total + part_ref[n].astype(jnp.float32)
        own = id_ref[...]
        for half in range(halves):
            shrink = total[:, half * rank : (half + 1) * rank]
            spread = jnp.concatenate(
                [jnp.where(own == a, shrink, 0.0).astype(jnp.bfloat16) for a in range(adapters)],
                axis=1,
            )
            matrix = weight_ref[:, half].reshape(adapters * rank, columns)
            out[:, half * columns : (half + 1) * columns] = jnp.dot(
                spread, matrix, preferred_element_type=jnp.float32
            ).astype(out.dtype)


def up(parts, ids, weight):
    count = len(ids)
    _, halves, _, columns = weight.shape
    whole = pl.BlockSpec(memory_space=pltpu.VMEM)
    return pl.pallas_call(
        lambda *refs: up_kernel(count, *refs),
        out_shape=[jax.ShapeDtypeStruct((i.shape[0], halves * columns), jnp.bfloat16) for i in ids],
        in_specs=[whole] * (1 + 2 * count),
        out_specs=[whole] * count,
        compiler_params=pltpu.CompilerParams(vmem_limit_bytes=VMEM),
        cost_estimate=SMALL,
        name="up",
    )(*ids, *parts, weight)


def base_kernel(x_ref, weight_ref, out_ref):
    out_ref[0] = jnp.dot(
        x_ref[...], weight_ref[...], preferred_element_type=jnp.float32
    ).astype(out_ref.dtype)


def base_blocks(x, weight, blocks, halves, columns):
    rows, width = x.shape
    return pl.pallas_call(
        base_kernel,
        out_shape=jax.ShapeDtypeStruct((blocks, rows, halves * columns), jnp.bfloat16),
        grid=(blocks, halves),
        in_specs=[
            pl.BlockSpec((rows, width), lambda b, k: (0, 0)),
            pl.BlockSpec((width, columns), lambda b, k: (0, k * blocks + b)),
        ],
        out_specs=pl.BlockSpec((1, rows, columns), lambda b, k: (b, 0, k)),
        compiler_params=pltpu.CompilerParams(vmem_limit_bytes=VMEM),
        cost_estimate=SMALL,
        name="base",
    )(x, weight)


def swap(x, axis, distance):
    count = lax.axis_size(axis)
    return lax.ppermute(x, axis, [(i, i ^ distance) for i in range(count)])


def together(*values):
    return lax.optimization_barrier(values)


def local(tokens, key_value_weight, adapter_down_weight, adapter_up_weight, row_adapter_index, ranks):
    steps, step_rows, width = tokens.shape
    inst_count = lax.axis_size("inst")
    tp_count = lax.axis_size("tp")
    held, _, rank2 = adapter_down_weight.shape
    halves, columns = adapter_up_weight.shape[1], adapter_up_weight.shape[3]
    rows = steps * step_rows
    me = lax.axis_index("inst")
    tp_me = lax.axis_index("tp")
    x = tokens.reshape(rows, width)
    ids = row_adapter_index.reshape(1, rows)
    chunk = 128
    pooled = inst_count == 4
    if pooled:
        own_cap, near_cap, far_cap, flex_cap = rows // 2, 448 * rows // 1024, rows // 4, 192 * rows // 1024
    else:
        own_cap = near_cap = far_cap = flex_cap = 0
    holder = ids // held
    base_near = own_cap
    base_far2 = base_near + near_cap
    base_flex = base_far2 + far_cap
    base_far3 = base_flex + flex_cap
    base_over = base_far3 + far_cap
    if pooled:
        cls = holder ^ me
        hit = (cls == jnp.arange(4)[:, None]).astype(jnp.bfloat16)
        earlier = (jnp.arange(rows)[:, None] < jnp.arange(rows)[None, :]).astype(jnp.bfloat16)
        before = jnp.dot(hit, earlier, preferred_element_type=jnp.float32).astype(jnp.int32)
        counts = jnp.sum(hit.astype(jnp.int32), axis=1)
        place = jnp.sum(jnp.where(hit > 0, before, 0), axis=0, keepdims=True)
        over_near = jnp.maximum(counts[1] - near_cap, 0)
        extra2 = jnp.maximum(counts[2] - far_cap, 0)
        extra3 = jnp.maximum(counts[3] - far_cap, 0)
        over_far = jnp.maximum(extra2 + extra3 - flex_cap, 0)
        flex = place - far_cap + jnp.where(cls == 3, extra2, 0)
        far_target = jnp.where(
            place < far_cap,
            place + jnp.where(cls == 2, base_far2, base_far3),
            jnp.where(flex < flex_cap, flex + base_flex, flex - flex_cap + over_near + base_over),
        )
        near_target = jnp.where(
            place < near_cap, place + base_near, place - near_cap + base_over
        )
        target = jnp.where(cls == 0, place, jnp.where(cls == 1, near_target, far_target))
        over = over_near + over_far
    else:
        target = jnp.arange(rows)[None, :]
        over = jnp.int32(rows)
    target_column = target.reshape(rows, 1)
    ids_column = ids.reshape(rows, 1)

    def slot_ids(start, size):
        sel = target_column == (start + jnp.arange(size))[None, :]
        return jnp.sum(jnp.where(sel, ids_column + 1, 0), axis=0, keepdims=True) - 1

    def put(start, rows_back):
        sel = target_column == (start + jnp.arange(rows_back.shape[0]))[None, :]
        return jnp.dot(
            sel.astype(jnp.bfloat16), rows_back, preferred_element_type=jnp.float32
        )

    def held_ids(global_ids):
        local_ids = global_ids.reshape(-1, 1) - me * held
        return jnp.where((local_ids >= 0) & (local_ids < held), local_ids, -1)

    def exchange(part):
        return lax.all_gather(part, "tp", axis=0, tiled=False)

    def shrink(xs, list_ids):
        return down(xs, list_ids, adapter_down_weight, ranks)

    def expand(parts, list_ids):
        return up(parts, list_ids, adapter_up_weight)

    def base_parts(x):
        return base_blocks(x, key_value_weight, tp_count, halves, columns)

    def base_send(parts):
        return lax.all_to_all(parts, "tp", 0, 0, tiled=True)

    def base_sum(parts):
        return jnp.sum(parts.astype(jnp.float32), axis=0)

    def largest(value, axis):
        count = lax.axis_size(axis)
        most = value
        for d in range(1, count):
            most = jnp.maximum(
                most, lax.ppermute(value, axis, [(i, (i + d) % count) for i in range(count)])
            )
        return most

    def add_overflow(total, trips):
        def more(carry):
            return carry[0] < trips

        def one(carry):
            trip, total = carry
            start = base_over + trip * chunk
            (mine,) = gather([0], [chunk], target - start, x)
            x_all = lax.all_gather(mine, "inst", axis=0, tiled=True)
            ids_all = held_ids(lax.all_gather(slot_ids(start, chunk), "inst", axis=0, tiled=True))
            (part,) = shrink([x_all], [ids_all])
            (delta,) = expand([exchange(part)], [ids_all])
            back = lax.all_to_all(
                delta.reshape(inst_count, chunk, halves * columns), "inst", 0, 0, tiled=True
            )
            mine = jnp.sum(back.astype(jnp.float32), axis=0).astype(jnp.bfloat16)
            return trip + 1, total + put(start, mine)

        return lax.while_loop(more, one, (jnp.int32(0), total))[1]

    if not pooled:
        trips = (largest(largest(over, "inst"), "groups") + chunk - 1) // chunk
        total = add_overflow(base_sum(base_send(base_parts(x))), trips)
        return total.astype(jnp.bfloat16).reshape(steps, step_rows, halves, columns)

    half = far_cap // 2
    (g_flex,) = gather([base_flex], [flex_cap], target, x)
    r_flex = swap(g_flex, "inst", 2)
    x, target, _ = together(x, target, g_flex)
    g_3a, g_near = gather([base_far3, base_near], [half, near_cap], target, x)
    r_3a = swap(g_3a, "inst", 3)
    r_near = swap(g_near, "inst", 1)

    all_ids = slot_ids(0, base_over)
    over = jnp.full((1, 1), over, jnp.int32)
    got1 = swap(jnp.concatenate([all_ids[:, base_near:base_far2], over], axis=1), "inst", 1)
    got2 = swap(jnp.concatenate([all_ids[:, base_far2:base_far3], over], axis=1), "inst", 2)
    got3 = swap(jnp.concatenate([all_ids[:, base_flex:base_over], over], axis=1), "inst", 3)
    most = jnp.max(jnp.concatenate([over] + [g[:, -1:] for g in (got1, got2, got3)], axis=1))
    trips = (largest(most, "groups") + chunk - 1) // chunk
    k_1, k_2, k_3 = held_ids(got1[:, :-1]), held_ids(got2[:, :-1]), held_ids(got3[:, :-1])
    k_2a, k_2b, k_flex = k_2[:half], k_2[half:far_cap], k_2[far_cap:]
    k_on, k_3a, k_3b = k_3[:flex_cap], k_3[flex_cap : flex_cap + half], k_3[flex_cap + half :]
    k_own = held_ids(all_ids[:, :own_cap])

    x, target, *_ = together(x, target, g_3a, g_near)
    parts = base_parts(x)
    base = base_send(parts)
    x, target, _ = together(x, target, parts)
    g_own, g_2a, g_3b, g_2b = gather(
        [0, base_far2, base_far3 + half, base_far2 + half], [own_cap] + [half] * 3, target, x
    )
    (s_own,) = shrink([g_own], [k_own])
    e_own = exchange(s_own)

    r_flex, s_own, g_2a, trips, k_flex, k_1, k_3a = together(
        r_flex, s_own, g_2a, trips, k_flex, k_1, k_3a
    )
    r_on = swap(r_flex, "inst", 1)
    r_2a = swap(g_2a, "inst", 2)
    (s_flex,) = shrink([r_flex], [k_flex])
    e_flex = exchange(s_flex)

    r_3a, r_near, g_3b, e_own, s_flex = together(r_3a, r_near, g_3b, e_own, s_flex)
    r_3b = swap(g_3b, "inst", 3)
    s_3a, s_near = shrink([r_3a, r_near], [k_3a, k_1])
    e_3a, e_near = exchange(s_3a), exchange(s_near)
    d_own, d_flex = expand([e_own, together(e_flex, s_3a)[0]], [k_own, k_flex])

    r_2a, r_on, g_2b, e_3a, e_near, d_own = together(r_2a, r_on, g_2b, e_3a, e_near, d_own)
    r_2b = swap(g_2b, "inst", 2)
    d_3a, d_near = expand([e_3a, e_near], [k_3a, k_1])
    b_3a, b_near = swap(d_3a, "inst", 3), swap(d_near, "inst", 1)
    r_2a, r_on, *_ = together(r_2a, r_on, d_3a)
    s_2a, s_on = shrink([r_2a, r_on], [k_2a, k_on])
    e_2a, e_on = exchange(s_2a), exchange(s_on)

    r_3b, e_2a, e_on, base = together(r_3b, e_2a, e_on, base)
    d_2a, d_on = expand([e_2a, e_on], [k_2a, k_on])
    b_2a, b_on = swap(d_2a, "inst", 2), swap(d_on, "inst", 1)
    r_3b, _ = together(r_3b, d_2a)
    (s_3b,) = shrink([r_3b], [k_3b])
    e_3b = exchange(s_3b)
    total = add_overflow(base_sum(base) + put(0, d_own), trips)

    r_2b, e_3b, b_on, total, b_near, b_3a = together(r_2b, e_3b, b_on, total, b_near, b_3a)
    (d_3b,) = expand([e_3b], [k_3b])
    b_3b, b_flex = swap(d_3b, "inst", 3), swap(d_flex + b_on, "inst", 2)
    r_2b, _ = together(r_2b, d_3b)
    (s_2b,) = shrink([r_2b], [k_2b])
    (d_2b,) = expand([exchange(s_2b)], [k_2b])
    b_2b = swap(d_2b, "inst", 2)
    total = total + put(base_near, jnp.concatenate([b_near, b_2a], axis=0))
    total = total + put(base_flex, jnp.concatenate([b_flex, b_3a, b_3b], axis=0))
    total = total + put(base_far2 + half, b_2b)
    return total.astype(jnp.bfloat16).reshape(steps, step_rows, halves, columns)


def solution(mesh):
    placed = (
        P(None, ("groups", "inst"), "tp"),
        P("tp", None),
        P(("groups", "inst"), "tp", None),
        P(("groups", "inst"), None, None, "tp"),
        P(None, ("groups", "inst")),
        P(("groups", "inst")),
    )
    return jax.shard_map(
        local,
        mesh=mesh,
        in_specs=placed,
        out_specs=P(None, ("groups", "inst"), None, "tp"),
        check_vma=False,
    )
```

```python
import jax
import jax.numpy as jnp
from jax import lax
from jax.experimental import pallas as pl
from jax.experimental.pallas import tpu as pltpu
from jax.sharding import PartitionSpec as P

VMEM = 48 * 1024 * 1024
SMALL = pl.CostEstimate(flops=1024, bytes_accessed=1024, transcendentals=0)


def gather_kernel(starts, target_ref, x_ref, *outs):
    target = target_ref[...]
    for start, out in zip(starts, outs):
        slot = start + lax.broadcasted_iota(jnp.int32, (out.shape[0], 1), 0)
        sel = jnp.where(slot == target, 1.0, 0.0).astype(jnp.bfloat16)
        out[...] = jnp.dot(sel, x_ref[...], preferred_element_type=jnp.float32).astype(out.dtype)


def gather(starts, sizes, target, x):
    rows, width = x.shape
    tile = min(512, width)
    return pl.pallas_call(
        lambda *refs: gather_kernel(starts, *refs),
        out_shape=[jax.ShapeDtypeStruct((n, width), x.dtype) for n in sizes],
        grid=(width // tile,),
        in_specs=[
            pl.BlockSpec((1, rows), lambda c: (0, 0)),
            pl.BlockSpec((rows, tile), lambda c: (0, c)),
        ],
        out_specs=[pl.BlockSpec((n, tile), lambda c: (0, c)) for n in sizes],
        compiler_params=pltpu.CompilerParams(vmem_limit_bytes=VMEM),
        cost_estimate=SMALL,
        name="gather",
    )(target, x)


def spans(sizes):
    ends = [sum(sizes[: n + 1]) for n in range(len(sizes))]
    return [(end - size, end) for end, size in zip(ends, sizes)]


def down_kernel(count, ranks_ref, id_ref, *refs):
    xs, weight_ref, out_ref, total_ref = refs[:count], refs[count], refs[count + 1], refs[count + 2]
    adapter = pl.program_id(0)

    @pl.when(adapter == 0)
    def _():
        total_ref[...] = jnp.zeros_like(total_ref)

    for x_ref, (low, high) in zip(xs, spans([x.shape[0] for x in xs])):
        part = jnp.dot(x_ref[...], weight_ref[0], preferred_element_type=jnp.float32)
        column = lax.broadcasted_iota(jnp.int32, part.shape, 1) % (part.shape[1] // 2)
        keep = (id_ref[low:high] == adapter) & (column < ranks_ref[adapter])
        total_ref[low:high] += jnp.where(keep, part, 0.0)

    @pl.when(adapter == pl.num_programs(0) - 1)
    def _():
        out_ref[...] = total_ref[...].astype(out_ref.dtype)


def down(xs, ids, weight, ranks):
    adapters, width, rank2 = weight.shape
    rows = ids.shape[0]
    fixed = lambda a: (0, 0)
    return pl.pallas_call(
        lambda *refs: down_kernel(len(xs), *refs),
        out_shape=jax.ShapeDtypeStruct((rows, rank2), jnp.bfloat16),
        grid=(adapters,),
        in_specs=[pl.BlockSpec(memory_space=pltpu.SMEM), pl.BlockSpec((rows, 1), fixed)]
        + [pl.BlockSpec(x.shape, fixed) for x in xs]
        + [pl.BlockSpec((1, width, rank2), lambda a: (a, 0, 0))],
        out_specs=pl.BlockSpec((rows, rank2), fixed),
        scratch_shapes=[pltpu.VMEM((rows, rank2), jnp.float32)],
        compiler_params=pltpu.CompilerParams(vmem_limit_bytes=VMEM),
        cost_estimate=SMALL,
        name="down",
    )(ranks, ids, *xs, weight)


def up_kernel(count, id_ref, *refs):
    parts, weight_ref, outs = refs[:count], refs[count], refs[count + 1 :]
    adapters, halves, rank, columns = weight_ref.shape
    for out, (low, high) in zip(outs, spans([out.shape[0] for out in outs])):
        terms = [p[low:high] if len(p.shape) == 2 else p[n, low:high] for p in parts for n in range(p.shape[0] if len(p.shape) == 3 else 1)]
        total = terms[0].astype(jnp.float32)
        for term in terms[1:]:
            total = total + term.astype(jnp.float32)
        own = id_ref[low:high]
        for half in range(halves):
            shrink = total[:, half * rank : (half + 1) * rank]
            spread = jnp.concatenate(
                [jnp.where(own == a, shrink, 0.0).astype(jnp.bfloat16) for a in range(adapters)],
                axis=1,
            )
            matrix = weight_ref[:, half].reshape(adapters * rank, columns)
            out[:, half * columns : (half + 1) * columns] = jnp.dot(
                spread, matrix, preferred_element_type=jnp.float32
            ).astype(out.dtype)


def up(parts, ids, sizes, weight):
    _, halves, _, columns = weight.shape
    whole = pl.BlockSpec(memory_space=pltpu.VMEM)
    return pl.pallas_call(
        lambda *refs: up_kernel(len(parts), *refs),
        out_shape=[jax.ShapeDtypeStruct((n, halves * columns), jnp.bfloat16) for n in sizes],
        in_specs=[whole] * (2 + len(parts)),
        out_specs=[whole] * len(sizes),
        compiler_params=pltpu.CompilerParams(vmem_limit_bytes=VMEM),
        cost_estimate=SMALL,
        name="up",
    )(ids, *parts, weight)


def base_kernel(order_ref, x_ref, weight_ref, *outs):
    part = jnp.dot(x_ref[...], weight_ref[...], preferred_element_type=jnp.float32)
    if len(outs) == 1:
        outs[0][0] = part.astype(outs[0].dtype)
    else:
        share = pl.num_programs(0) // len(outs)
        for n, out in enumerate(outs):

            @pl.when(pl.program_id(0) // share == n)
            def _():
                out[0] = part.astype(out.dtype)


def base_blocks(x, weight, order, outputs, halves, columns, piece=0, pieces=1):
    rows, width = x.shape[0] // pieces, x.shape[1]
    blocks = order.shape[0]
    share = blocks // outputs

    def place(n):
        return lambda b, k, o: (
            jnp.clip(b - n * share, 0, share - 1),
            0,
            jnp.where(b < n * share, 0, jnp.where(b >= (n + 1) * share, halves - 1, k)),
        )

    return pl.pallas_call(
        base_kernel,
        out_shape=[jax.ShapeDtypeStruct((share, rows, halves * columns), jnp.bfloat16)] * outputs,
        grid_spec=pltpu.PrefetchScalarGridSpec(
            num_scalar_prefetch=1,
            grid=(blocks, halves),
            in_specs=[
                pl.BlockSpec((rows, width), lambda b, k, o: (piece, 0)),
                pl.BlockSpec((width, columns), lambda b, k, o: (0, k * blocks + o[b])),
            ],
            out_specs=[pl.BlockSpec((1, rows, columns), place(n)) for n in range(outputs)],
        ),
        compiler_params=pltpu.CompilerParams(vmem_limit_bytes=VMEM),
        cost_estimate=SMALL,
        name="base",
    )(order, x, weight)


def finish_kernel(starts, total_ref, target_ref, *refs):
    target, out_ref = target_ref[...], refs[-1]
    total = total_ref[...]
    for start, list_ref in zip(starts, refs):
        slot = start + lax.broadcasted_iota(jnp.int32, (1, list_ref.shape[0]), 1)
        sel = jnp.where(target == slot, 1.0, 0.0).astype(jnp.bfloat16)
        total = total + jnp.dot(sel, list_ref[...], preferred_element_type=jnp.float32)
    out_ref[...] = total.astype(out_ref.dtype)


def finish(total, target, starts, lists):
    rows, columns = total.shape
    tile = rows // 4
    return pl.pallas_call(
        lambda *refs: finish_kernel(starts, *refs),
        out_shape=jax.ShapeDtypeStruct((rows, columns), jnp.bfloat16),
        grid=(rows // tile,),
        in_specs=[
            pl.BlockSpec((tile, columns), lambda r: (r, 0)),
            pl.BlockSpec((tile, 1), lambda r: (r, 0)),
        ]
        + [pl.BlockSpec(part.shape, lambda r: (0, 0)) for part in lists],
        out_specs=pl.BlockSpec((tile, columns), lambda r: (r, 0)),
        compiler_params=pltpu.CompilerParams(vmem_limit_bytes=VMEM),
        cost_estimate=SMALL,
        name="finish",
    )(total, target, *lists)


def swap(x, axis, distance):
    count = lax.axis_size(axis)
    return lax.ppermute(x, axis, [(i, i ^ distance) for i in range(count)])


def together(*values):
    return lax.optimization_barrier(values)


def local(tokens, key_value_weight, adapter_down_weight, adapter_up_weight, row_adapter_index, ranks):
    steps, step_rows, width = tokens.shape
    inst_count = lax.axis_size("inst")
    tp_count = lax.axis_size("tp")
    held, _, rank2 = adapter_down_weight.shape
    halves, columns = adapter_up_weight.shape[1], adapter_up_weight.shape[3]
    rows = steps * step_rows
    me = lax.axis_index("inst")
    tp_me = lax.axis_index("tp")
    x = tokens.reshape(rows, width)
    ids = row_adapter_index.reshape(1, rows)
    chunk = 64
    pooled = inst_count == 4
    if pooled:
        own_cap, near_cap, far_cap, flex_cap = rows // 2, 448 * rows // 1024, 224 * rows // 1024, 288 * rows // 1024
    else:
        own_cap = near_cap = far_cap = flex_cap = 0
    holder = ids // held
    base_near = own_cap
    base_far2 = base_near + near_cap
    base_flex = base_far2 + far_cap
    base_far3 = base_flex + flex_cap
    base_over = base_far3 + far_cap
    if pooled:
        cls = holder ^ me
        hit = (cls == jnp.arange(4)[:, None]).astype(jnp.bfloat16)
        earlier = (jnp.arange(rows)[:, None] < jnp.arange(rows)[None, :]).astype(jnp.bfloat16)
        before = jnp.dot(hit, earlier, preferred_element_type=jnp.float32).astype(jnp.int32)
        counts = jnp.sum(hit.astype(jnp.int32), axis=1)
        place = jnp.sum(jnp.where(hit > 0, before, 0), axis=0, keepdims=True)
        over_near = jnp.maximum(counts[1] - near_cap, 0)
        extra2 = jnp.maximum(counts[2] - far_cap, 0)
        extra3 = jnp.maximum(counts[3] - far_cap, 0)
        over_far = jnp.maximum(extra2 + extra3 - flex_cap, 0)
        flex = place - far_cap + jnp.where(cls == 3, extra2, 0)
        far_target = jnp.where(
            place < far_cap,
            place + jnp.where(cls == 2, base_far2, base_far3),
            jnp.where(flex < flex_cap, flex + base_flex, flex - flex_cap + over_near + base_over),
        )
        near_target = jnp.where(
            place < near_cap, place + base_near, place - near_cap + base_over
        )
        target = jnp.where(cls == 0, place, jnp.where(cls == 1, near_target, far_target))
        over = over_near + over_far
    else:
        target = jnp.arange(rows)[None, :]
        over = jnp.int32(rows)
    target_column = target.reshape(rows, 1)
    ids_column = ids.reshape(rows, 1)

    def slot_ids(start, size):
        sel = target_column == (start + jnp.arange(size))[None, :]
        return jnp.sum(jnp.where(sel, ids_column + 1, 0), axis=0, keepdims=True) - 1

    def put(start, rows_back):
        sel = target_column == (start + jnp.arange(rows_back.shape[0]))[None, :]
        return jnp.dot(
            sel.astype(jnp.bfloat16), rows_back, preferred_element_type=jnp.float32
        )

    def held_ids(global_ids):
        local_ids = global_ids.reshape(-1, 1) - me * held
        return jnp.where((local_ids >= 0) & (local_ids < held), local_ids, -1)

    def add(a, b):
        return (a.astype(jnp.float32) + b.astype(jnp.float32)).astype(jnp.bfloat16)

    def gathered(part):
        return lax.all_gather(part, "tp", axis=0, tiled=False)

    def exchange(part):
        if tp_count != 4:
            return [lax.psum(part.astype(jnp.float32), "tp")]
        pair = add(part, swap(part, "tp", 1))
        return [pair, swap(pair, "tp", 2)]

    def shrink(xs, list_ids):
        return down(xs, list_ids, adapter_down_weight, ranks)

    def expand(parts, list_ids, sizes):
        return up(parts, list_ids, sizes, adapter_up_weight)

    def base_parts(x):
        order = jnp.arange(tp_count, dtype=jnp.int32)
        (part,) = base_blocks(x, key_value_weight, order, 1, halves, columns)
        return part

    def base_sent(part):
        return lax.all_to_all(part, "tp", 0, 0, tiled=True)

    def largest(value, axis):
        count = lax.axis_size(axis)
        most = value
        for d in range(1, count):
            most = jnp.maximum(
                most, lax.ppermute(value, axis, [(i, (i + d) % count) for i in range(count)])
            )
        return most

    def add_overflow(total, trips):
        def more(carry):
            return carry[0] < trips

        def one(carry):
            trip, total = carry
            start = base_over + trip * chunk
            (mine,) = gather([0], [chunk], target - start, x)
            x_all = lax.all_gather(mine, "inst", axis=0, tiled=True)
            ids_all = held_ids(lax.all_gather(slot_ids(start, chunk), "inst", axis=0, tiled=True))
            part = exchange(shrink([x_all], ids_all))
            (delta,) = expand(part, ids_all, [inst_count * chunk])
            back = lax.all_to_all(
                delta.reshape(inst_count, chunk, halves * columns), "inst", 0, 0, tiled=True
            )
            mine = jnp.sum(back.astype(jnp.float32), axis=0).astype(jnp.bfloat16)
            return trip + 1, total + put(start, mine)

        return lax.while_loop(more, one, (jnp.int32(0), total))[1]

    if not pooled:
        trips = (largest(largest(over, "inst"), "groups") + chunk - 1) // chunk
        total = add_overflow(
            jnp.sum(base_sent(base_parts(x)).astype(jnp.float32), axis=0), trips
        )
        return total.astype(jnp.bfloat16).reshape(steps, step_rows, halves, columns)

    all_ids = slot_ids(0, base_over)
    over = jnp.full((1, 1), over, jnp.int32)
    got1 = swap(jnp.concatenate([all_ids[:, base_near:base_far2], over], axis=1), "inst", 1)
    got2 = swap(jnp.concatenate([all_ids[:, base_far2:base_far3], over], axis=1), "inst", 2)
    got3 = swap(jnp.concatenate([all_ids[:, base_flex:base_over], over], axis=1), "inst", 3)

    target, got1, got2, got3 = together(target, got1, got2, got3)
    (g_flex,) = gather([base_flex], [flex_cap], target, x)
    r_flex = swap(g_flex, "inst", 2)
    x, target, _ = together(x, target, g_flex)
    (g_near,) = gather([base_near], [near_cap], target, x)
    r_near = swap(g_near, "inst", 1)
    most = jnp.max(jnp.concatenate([over] + [g[:, -1:] for g in (got1, got2, got3)], axis=1))
    trips = (largest(most, "groups") + chunk - 1) // chunk
    k_1, k_2, k_3 = held_ids(got1[:, :-1]), held_ids(got2[:, :-1]), held_ids(got3[:, :-1])
    k_2, k_flex = k_2[:far_cap], k_2[far_cap:]
    k_on, k_3 = k_3[:flex_cap], k_3[flex_cap:]
    k_own = held_ids(all_ids[:, :own_cap])
    k_on_2 = jnp.concatenate([k_on, k_2], axis=0)

    x, target, _ = together(x, target, g_near)
    g_3, g_own, g_2 = gather(
        [base_far3, 0, base_far2], [far_cap, own_cap, far_cap], target, x
    )
    x, g_own = together(x, g_own)
    part = base_parts(x)
    sent = base_sent(part)

    r_flex, g_3, g_2, trips, k_flex, k_own, k_on_2, k_on, k_3, k_1, k_2, _ = together(
        r_flex, g_3, g_2, trips, k_flex, k_own, k_on_2, k_on, k_3, k_1, k_2, part
    )
    r_3 = swap(g_3, "inst", 3)
    r_on = swap(r_flex, "inst", 1)
    s_flex = shrink([r_flex], k_flex)
    g_own, s_flex = together(g_own, s_flex)
    s_own = shrink([g_own], k_own)
    (d_flex,) = expand([gathered(s_flex)], k_flex, [flex_cap])

    r_3, g_2, s_own, d_flex = together(r_3, g_2, s_own, d_flex)
    r_2 = swap(g_2, "inst", 2)
    s_3 = shrink([r_3], k_3)
    (d_3,) = expand([gathered(s_3)], k_3, [far_cap])
    b_3 = swap(d_3, "inst", 3)

    r_near, d_3 = together(r_near, d_3)
    s_near = shrink([r_near], k_1)
    (d_near,) = expand([gathered(s_near)], k_1, [near_cap])
    b_near = swap(d_near, "inst", 1)

    r_on, r_2, d_near = together(r_on, r_2, d_near)
    s_on_2 = shrink([r_on, r_2], k_on_2)
    s_on, s_2 = s_on_2[:flex_cap], s_on_2[flex_cap:]
    (d_on,) = expand([gathered(s_on)], k_on, [flex_cap])
    b_on = swap(d_on, "inst", 1)
    s_2, d_on, b_3, b_near, sent = together(s_2, d_on, b_3, b_near, sent)
    (d_2,) = expand([gathered(s_2)], k_2, [far_cap])
    b_2 = swap(d_2, "inst", 2)
    b_on, d_2 = together(b_on, d_2)
    back_flex = d_flex + b_on
    b_flex = swap(back_flex, "inst", 2)
    s_own, sent, b_3, b_near, _ = together(s_own, sent, b_3, b_near, back_flex)
    (d_own,) = expand([gathered(s_own)], k_own, [own_cap])
    base = jnp.sum(sent.astype(jnp.float32), axis=0)
    total = add_overflow(base + put(0, jnp.concatenate([d_own, b_near], axis=0)), trips)
    total = total + put(base_far3, b_3)
    total = finish(total, target_column, [base_far2, base_flex], [b_2, b_flex])
    return total.reshape(steps, step_rows, halves, columns)


def solution(mesh):
    placed = (
        P(None, ("groups", "inst"), "tp"),
        P("tp", None),
        P(("groups", "inst"), "tp", None),
        P(("groups", "inst"), None, None, "tp"),
        P(None, ("groups", "inst")),
        P(("groups", "inst")),
    )
    return jax.shard_map(
        local,
        mesh=mesh,
        in_specs=placed,
        out_specs=P(None, ("groups", "inst"), None, "tp"),
        check_vma=False,
    )
```

```python
import jax
import jax.numpy as jnp
from jax import lax
from jax.experimental import pallas as pl
from jax.experimental.pallas import tpu as pltpu
from jax.sharding import PartitionSpec as P

VMEM = 48 * 1024 * 1024
SMALL = pl.CostEstimate(flops=1024, bytes_accessed=1024, transcendentals=0)


def gather_kernel(starts, target_ref, x_ref, *outs):
    target = target_ref[...]
    for start, out in zip(starts, outs):
        slot = start + lax.broadcasted_iota(jnp.int32, (out.shape[0], 1), 0)
        sel = jnp.where(slot == target, 1.0, 0.0).astype(jnp.bfloat16)
        out[...] = jnp.dot(sel, x_ref[...], preferred_element_type=jnp.float32).astype(out.dtype)


def gather(starts, sizes, target, x):
    rows, width = x.shape
    tile = min(512, width)
    return pl.pallas_call(
        lambda *refs: gather_kernel(starts, *refs),
        out_shape=[jax.ShapeDtypeStruct((n, width), x.dtype) for n in sizes],
        grid=(width // tile,),
        in_specs=[
            pl.BlockSpec((1, rows), lambda c: (0, 0)),
            pl.BlockSpec((rows, tile), lambda c: (0, c)),
        ],
        out_specs=[pl.BlockSpec((n, tile), lambda c: (0, c)) for n in sizes],
        compiler_params=pltpu.CompilerParams(vmem_limit_bytes=VMEM),
        cost_estimate=SMALL,
        name="gather",
    )(target, x)


def spans(sizes):
    ends = [sum(sizes[: n + 1]) for n in range(len(sizes))]
    return [(end - size, end) for end, size in zip(ends, sizes)]


def down_kernel(count, ranks_ref, id_ref, *refs):
    xs, weight_ref, out_ref, total_ref = refs[:count], refs[count], refs[count + 1], refs[count + 2]
    adapter = pl.program_id(0)

    @pl.when(adapter == 0)
    def _():
        total_ref[...] = jnp.zeros_like(total_ref)

    for x_ref, (low, high) in zip(xs, spans([x.shape[0] for x in xs])):
        kept = total_ref[low:high]
        for n in range(weight_ref.shape[0]):
            mine = adapter * weight_ref.shape[0] + n
            part = jnp.dot(x_ref[...], weight_ref[n], preferred_element_type=jnp.float32)
            column = lax.broadcasted_iota(jnp.int32, part.shape, 1) % (part.shape[1] // 2)
            keep = (id_ref[low:high] == mine) & (column < ranks_ref[mine])
            kept = jnp.where(keep, part, kept)
        total_ref[low:high] = kept

    @pl.when(adapter == pl.num_programs(0) - 1)
    def _():
        out_ref[...] = total_ref[...].astype(out_ref.dtype)


def down(xs, ids, weight, ranks):
    adapters, width, rank2 = weight.shape
    rows = ids.shape[0]
    fixed = lambda a: (0, 0)
    return pl.pallas_call(
        lambda *refs: down_kernel(len(xs), *refs),
        out_shape=jax.ShapeDtypeStruct((rows, rank2), jnp.bfloat16),
        grid=(adapters // 2,),
        in_specs=[pl.BlockSpec(memory_space=pltpu.SMEM), pl.BlockSpec((rows, 1), fixed)]
        + [pl.BlockSpec(x.shape, fixed) for x in xs]
        + [pl.BlockSpec((2, width, rank2), lambda a: (a, 0, 0))],
        out_specs=pl.BlockSpec((rows, rank2), fixed),
        scratch_shapes=[pltpu.VMEM((rows, rank2), jnp.float32)],
        compiler_params=pltpu.CompilerParams(vmem_limit_bytes=VMEM),
        cost_estimate=SMALL,
        name="down",
    )(ranks, ids, *xs, weight)


def up_kernel(count, id_ref, *refs):
    parts, weight_ref, outs = refs[:count], refs[count], refs[count + 1 :]
    adapters, halves, rank, columns = weight_ref.shape
    for out, (low, high) in zip(outs, spans([out.shape[0] for out in outs])):
        terms = [p[low:high] if len(p.shape) == 2 else p[n, low:high] for p in parts for n in range(p.shape[0] if len(p.shape) == 3 else 1)]
        total = terms[0].astype(jnp.float32)
        for term in terms[1:]:
            total = total + term.astype(jnp.float32)
        own = id_ref[low:high]
        for half in range(halves):
            shrink = total[:, half * rank : (half + 1) * rank]
            spread = jnp.concatenate(
                [jnp.where(own == a, shrink, 0.0).astype(jnp.bfloat16) for a in range(adapters)],
                axis=1,
            )
            matrix = weight_ref[:, half].reshape(adapters * rank, columns)
            out[:, half * columns : (half + 1) * columns] = jnp.dot(
                spread, matrix, preferred_element_type=jnp.float32
            ).astype(out.dtype)


def up(parts, ids, sizes, weight):
    _, halves, _, columns = weight.shape
    whole = pl.BlockSpec(memory_space=pltpu.VMEM)
    return pl.pallas_call(
        lambda *refs: up_kernel(len(parts), *refs),
        out_shape=[jax.ShapeDtypeStruct((n, halves * columns), jnp.bfloat16) for n in sizes],
        in_specs=[whole] * (2 + len(parts)),
        out_specs=[whole] * len(sizes),
        compiler_params=pltpu.CompilerParams(vmem_limit_bytes=VMEM),
        cost_estimate=SMALL,
        name="up",
    )(ids, *parts, weight)


def base_kernel(order_ref, x_ref, weight_ref, *outs):
    part = jnp.dot(x_ref[...], weight_ref[...], preferred_element_type=jnp.float32)
    if len(outs) == 1:
        outs[0][0] = part.astype(outs[0].dtype)
    else:
        share = pl.num_programs(0) // len(outs)
        for n, out in enumerate(outs):

            @pl.when(pl.program_id(0) // share == n)
            def _():
                out[0] = part.astype(out.dtype)


def base_blocks(x, weight, order, outputs, halves, columns, piece=0, pieces=1):
    rows, width = x.shape[0] // pieces, x.shape[1]
    blocks = order.shape[0]
    share = blocks // outputs

    def place(n):
        return lambda b, k, o: (
            jnp.clip(b - n * share, 0, share - 1),
            0,
            jnp.where(b < n * share, 0, jnp.where(b >= (n + 1) * share, halves - 1, k)),
        )

    return pl.pallas_call(
        base_kernel,
        out_shape=[jax.ShapeDtypeStruct((share, rows, halves * columns), jnp.bfloat16)] * outputs,
        grid_spec=pltpu.PrefetchScalarGridSpec(
            num_scalar_prefetch=1,
            grid=(blocks, halves),
            in_specs=[
                pl.BlockSpec((rows, width), lambda b, k, o: (piece, 0)),
                pl.BlockSpec((width, columns), lambda b, k, o: (0, k * blocks + o[b])),
            ],
            out_specs=[pl.BlockSpec((1, rows, columns), place(n)) for n in range(outputs)],
        ),
        compiler_params=pltpu.CompilerParams(vmem_limit_bytes=VMEM),
        cost_estimate=SMALL,
        name="base",
    )(order, x, weight)


def finish_kernel(starts, total_ref, target_ref, *refs):
    target, out_ref = target_ref[...], refs[-1]
    total = total_ref[...]
    for start, list_ref in zip(starts, refs):
        slot = start + lax.broadcasted_iota(jnp.int32, (1, list_ref.shape[0]), 1)
        sel = jnp.where(target == slot, 1.0, 0.0).astype(jnp.bfloat16)
        total = total + jnp.dot(sel, list_ref[...], preferred_element_type=jnp.float32)
    out_ref[...] = total.astype(out_ref.dtype)


def finish(total, target, starts, lists):
    rows, columns = total.shape
    tile = rows // 4
    return pl.pallas_call(
        lambda *refs: finish_kernel(starts, *refs),
        out_shape=jax.ShapeDtypeStruct((rows, columns), jnp.bfloat16),
        grid=(rows // tile,),
        in_specs=[
            pl.BlockSpec((tile, columns), lambda r: (r, 0)),
            pl.BlockSpec((tile, 1), lambda r: (r, 0)),
        ]
        + [pl.BlockSpec(part.shape, lambda r: (0, 0)) for part in lists],
        out_specs=pl.BlockSpec((tile, columns), lambda r: (r, 0)),
        compiler_params=pltpu.CompilerParams(vmem_limit_bytes=VMEM),
        cost_estimate=SMALL,
        name="finish",
    )(total, target, *lists)


def swap(x, axis, distance):
    count = lax.axis_size(axis)
    return lax.ppermute(x, axis, [(i, i ^ distance) for i in range(count)])


def together(*values):
    return lax.optimization_barrier(values)


def local(tokens, key_value_weight, adapter_down_weight, adapter_up_weight, row_adapter_index, ranks):
    steps, step_rows, width = tokens.shape
    inst_count = lax.axis_size("inst")
    tp_count = lax.axis_size("tp")
    held, _, rank2 = adapter_down_weight.shape
    halves, columns = adapter_up_weight.shape[1], adapter_up_weight.shape[3]
    rows = steps * step_rows
    me = lax.axis_index("inst")
    tp_me = lax.axis_index("tp")
    x = tokens.reshape(rows, width)
    ids = row_adapter_index.reshape(1, rows)
    chunk = 64
    pooled = inst_count == 4
    if pooled:
        own_cap, near_cap, far_cap, flex_cap = rows // 2, 448 * rows // 1024, 224 * rows // 1024, 288 * rows // 1024
    else:
        own_cap = near_cap = far_cap = flex_cap = 0
    holder = ids // held
    base_near = own_cap
    base_far2 = base_near + near_cap
    base_flex = base_far2 + far_cap
    base_far3 = base_flex + flex_cap
    base_over = base_far3 + far_cap
    if pooled:
        cls = holder ^ me
        hit = (cls == jnp.arange(4)[:, None]).astype(jnp.bfloat16)
        earlier = (jnp.arange(rows)[:, None] < jnp.arange(rows)[None, :]).astype(jnp.bfloat16)
        before = jnp.dot(hit, earlier, preferred_element_type=jnp.float32).astype(jnp.int32)
        counts = jnp.sum(hit.astype(jnp.int32), axis=1)
        place = jnp.sum(jnp.where(hit > 0, before, 0), axis=0, keepdims=True)
        over_near = jnp.maximum(counts[1] - near_cap, 0)
        extra2 = jnp.maximum(counts[2] - far_cap, 0)
        extra3 = jnp.maximum(counts[3] - far_cap, 0)
        over_far = jnp.maximum(extra2 + extra3 - flex_cap, 0)
        flex = place - far_cap + jnp.where(cls == 3, extra2, 0)
        far_target = jnp.where(
            place < far_cap,
            place + jnp.where(cls == 2, base_far2, base_far3),
            jnp.where(flex < flex_cap, flex + base_flex, flex - flex_cap + over_near + base_over),
        )
        near_target = jnp.where(
            place < near_cap, place + base_near, place - near_cap + base_over
        )
        target = jnp.where(cls == 0, place, jnp.where(cls == 1, near_target, far_target))
        over = over_near + over_far
    else:
        target = jnp.arange(rows)[None, :]
        over = jnp.int32(rows)
    target_column = target.reshape(rows, 1)
    ids_column = ids.reshape(rows, 1)

    def slot_ids(start, size):
        sel = target_column == (start + jnp.arange(size))[None, :]
        return jnp.sum(jnp.where(sel, ids_column + 1, 0), axis=0, keepdims=True) - 1

    def put(start, rows_back):
        sel = target_column == (start + jnp.arange(rows_back.shape[0]))[None, :]
        return jnp.dot(
            sel.astype(jnp.bfloat16), rows_back, preferred_element_type=jnp.float32
        )

    def held_ids(global_ids):
        local_ids = global_ids.reshape(-1, 1) - me * held
        return jnp.where((local_ids >= 0) & (local_ids < held), local_ids, -1)

    def add(a, b):
        return (a.astype(jnp.float32) + b.astype(jnp.float32)).astype(jnp.bfloat16)

    def gathered(part):
        return lax.all_gather(part, "tp", axis=0, tiled=False)

    def exchange(part):
        if tp_count != 4:
            return [lax.psum(part.astype(jnp.float32), "tp")]
        pair = add(part, swap(part, "tp", 1))
        return [pair, swap(pair, "tp", 2)]

    def shrink(xs, list_ids):
        return down(xs, list_ids, adapter_down_weight, ranks)

    def expand(parts, list_ids, sizes):
        return up(parts, list_ids, sizes, adapter_up_weight)

    def base_parts(x):
        order = jnp.arange(tp_count, dtype=jnp.int32)
        (part,) = base_blocks(x, key_value_weight, order, 1, halves, columns)
        return part

    def base_sent(part):
        return lax.all_to_all(part, "tp", 0, 0, tiled=True)

    def largest(value, axis):
        count = lax.axis_size(axis)
        most = value
        for d in range(1, count):
            most = jnp.maximum(
                most, lax.ppermute(value, axis, [(i, (i + d) % count) for i in range(count)])
            )
        return most

    def add_overflow(total, trips):
        def more(carry):
            return carry[0] < trips

        def one(carry):
            trip, total = carry
            start = base_over + trip * chunk
            (mine,) = gather([0], [chunk], target - start, x)
            x_all = lax.all_gather(mine, "inst", axis=0, tiled=True)
            ids_all = held_ids(lax.all_gather(slot_ids(start, chunk), "inst", axis=0, tiled=True))
            part = exchange(shrink([x_all], ids_all))
            (delta,) = expand(part, ids_all, [inst_count * chunk])
            back = lax.all_to_all(
                delta.reshape(inst_count, chunk, halves * columns), "inst", 0, 0, tiled=True
            )
            mine = jnp.sum(back.astype(jnp.float32), axis=0).astype(jnp.bfloat16)
            return trip + 1, total + put(start, mine)

        return lax.while_loop(more, one, (jnp.int32(0), total))[1]

    if not pooled:
        trips = (largest(largest(over, "inst"), "groups") + chunk - 1) // chunk
        total = add_overflow(
            jnp.sum(base_sent(base_parts(x)).astype(jnp.float32), axis=0), trips
        )
        return total.astype(jnp.bfloat16).reshape(steps, step_rows, halves, columns)

    all_ids = slot_ids(0, base_over)
    over = jnp.full((1, 1), over, jnp.int32)
    got1 = swap(jnp.concatenate([all_ids[:, base_near:base_far2], over], axis=1), "inst", 1)
    got2 = swap(jnp.concatenate([all_ids[:, base_far2:base_far3], over], axis=1), "inst", 2)
    got3 = swap(jnp.concatenate([all_ids[:, base_flex:base_over], over], axis=1), "inst", 3)

    target, got1, got2, got3 = together(target, got1, got2, got3)
    (g_flex,) = gather([base_flex], [flex_cap], target, x)
    r_flex = swap(g_flex, "inst", 2)
    x, target, _ = together(x, target, g_flex)
    near = near_cap // 2
    (g_na,) = gather([base_near], [near], target, x)
    r_na = swap(g_na, "inst", 1)
    most = jnp.max(jnp.concatenate([over] + [g[:, -1:] for g in (got1, got2, got3)], axis=1))
    trips = (largest(most, "groups") + chunk - 1) // chunk
    k_1, k_2, k_3 = held_ids(got1[:, :-1]), held_ids(got2[:, :-1]), held_ids(got3[:, :-1])
    k_2, k_flex = k_2[:far_cap], k_2[far_cap:]
    k_on, k_3 = k_3[:flex_cap], k_3[flex_cap:]
    k_own = held_ids(all_ids[:, :own_cap])
    k_na, k_nb = k_1[:near_cap // 2], k_1[near_cap // 2 :]
    k_3_na = jnp.concatenate([k_3, k_na], axis=0)
    k_2_nb = jnp.concatenate([k_2, k_nb], axis=0)

    x, target, _ = together(x, target, g_na)
    g_3, g_own, g_2, g_nb = gather(
        [base_far3, 0, base_far2, base_near + near], [far_cap, own_cap, far_cap, near], target, x
    )
    x, g_own = together(x, g_own)
    part = base_parts(x)
    sent = base_sent(part)

    r_flex, r_na, g_3, g_2, g_nb, trips, k_flex, k_own, k_on, k_3_na, k_2_nb, _ = together(
        r_flex, r_na, g_3, g_2, g_nb, trips, k_flex, k_own, k_on, k_3_na, k_2_nb, part
    )
    r_3 = swap(g_3, "inst", 3)
    r_on = swap(r_flex, "inst", 1)
    s_flex = shrink([r_flex], k_flex)
    g_own, s_flex = together(g_own, s_flex)
    s_own = shrink([g_own], k_own)
    s_flex, s_own = together(s_flex, s_own)
    (d_flex,) = expand([gathered(s_flex)], k_flex, [flex_cap])

    r_3, r_na, g_2, g_nb, s_own, d_flex = together(r_3, r_na, g_2, g_nb, s_own, d_flex)
    r_2 = swap(g_2, "inst", 2)
    r_nb = swap(g_nb, "inst", 1)
    s_3_na = shrink([r_3, r_na], k_3_na)
    d_3, d_na = expand([gathered(s_3_na)], k_3_na, [far_cap, near])

    r_on, d_3, d_na = together(r_on, d_3, d_na)
    b_3, b_na = swap(d_3, "inst", 3), swap(d_na, "inst", 1)
    (d_on,) = expand([gathered(shrink([r_on], k_on))], k_on, [flex_cap])
    b_on = swap(d_on, "inst", 1)

    r_2, r_nb, d_on = together(r_2, r_nb, d_on)
    s_2_nb = shrink([r_2, r_nb], k_2_nb)
    s_2_nb, b_on = together(s_2_nb, b_on)
    back_flex = d_flex + b_on
    b_flex = swap(back_flex, "inst", 2)
    s_2_nb, _ = together(s_2_nb, back_flex)
    d_2, d_nb = expand([gathered(s_2_nb)], k_2_nb, [far_cap, near])
    d_2, d_nb, b_flex, b_3, b_na, e_own = together(d_2, d_nb, b_flex, b_3, b_na, gathered(s_own))
    b_2, b_nb = swap(d_2, "inst", 2), swap(d_nb, "inst", 1)
    e_own, sent, b_3, b_na, _ = together(e_own, sent, b_3, b_na, d_2)
    (d_own,) = expand([e_own], k_own, [own_cap])
    base = jnp.sum(sent.astype(jnp.float32), axis=0)
    total = add_overflow(base + put(0, jnp.concatenate([d_own, b_na], axis=0)), trips)
    total = total + put(base_far3, b_3)
    total = finish(
        total, target_column, [base_far2, base_flex, base_near + near], [b_2, b_flex, b_nb]
    )
    return total.reshape(steps, step_rows, halves, columns)


def solution(mesh):
    placed = (
        P(None, ("groups", "inst"), "tp"),
        P("tp", None),
        P(("groups", "inst"), "tp", None),
        P(("groups", "inst"), None, None, "tp"),
        P(None, ("groups", "inst")),
        P(("groups", "inst")),
    )
    return jax.shard_map(
        local,
        mesh=mesh,
        in_specs=placed,
        out_specs=P(None, ("groups", "inst"), None, "tp"),
        check_vma=False,
    )
```

```python
import jax
import jax.numpy as jnp
from jax import lax
from jax.experimental import pallas as pl
from jax.experimental.pallas import tpu as pltpu
from jax.sharding import PartitionSpec as P

VMEM = 48 * 1024 * 1024
SMALL = pl.CostEstimate(flops=1024, bytes_accessed=1024, transcendentals=0)


def gather_kernel(starts, target_ref, x_ref, *outs):
    target = target_ref[...]
    for start, out in zip(starts, outs):
        slot = start + lax.broadcasted_iota(jnp.int32, (out.shape[0], 1), 0)
        sel = jnp.where(slot == target, 1.0, 0.0).astype(jnp.bfloat16)
        out[...] = jnp.dot(sel, x_ref[...], preferred_element_type=jnp.float32).astype(out.dtype)


def gather(starts, sizes, target, x):
    rows, width = x.shape
    tile = min(512, width)
    return pl.pallas_call(
        lambda *refs: gather_kernel(starts, *refs),
        out_shape=[jax.ShapeDtypeStruct((n, width), x.dtype) for n in sizes],
        grid=(width // tile,),
        in_specs=[
            pl.BlockSpec((1, rows), lambda c: (0, 0)),
            pl.BlockSpec((rows, tile), lambda c: (0, c)),
        ],
        out_specs=[pl.BlockSpec((n, tile), lambda c: (0, c)) for n in sizes],
        compiler_params=pltpu.CompilerParams(vmem_limit_bytes=VMEM),
        cost_estimate=SMALL,
        name="gather",
    )(target, x)


def spans(sizes):
    ends = [sum(sizes[: n + 1]) for n in range(len(sizes))]
    return [(end - size, end) for end, size in zip(ends, sizes)]


def down_kernel(count, ranks_ref, id_ref, *refs):
    xs, weight_ref, out_ref, total_ref = refs[:count], refs[count], refs[count + 1], refs[count + 2]
    adapter = pl.program_id(0)

    @pl.when(adapter == 0)
    def _():
        total_ref[...] = jnp.zeros_like(total_ref)

    for x_ref, (low, high) in zip(xs, spans([x.shape[0] for x in xs])):
        kept = total_ref[low:high]
        for n in range(weight_ref.shape[0]):
            mine = adapter * weight_ref.shape[0] + n
            part = jnp.dot(x_ref[...], weight_ref[n], preferred_element_type=jnp.float32)
            column = lax.broadcasted_iota(jnp.int32, part.shape, 1) % (part.shape[1] // 2)
            keep = (id_ref[low:high] == mine) & (column < ranks_ref[mine])
            kept = jnp.where(keep, part, kept)
        total_ref[low:high] = kept

    @pl.when(adapter == pl.num_programs(0) - 1)
    def _():
        out_ref[...] = total_ref[...].astype(out_ref.dtype)


def down(xs, ids, weight, ranks):
    adapters, width, rank2 = weight.shape
    rows = ids.shape[0]
    fixed = lambda a: (0, 0)
    return pl.pallas_call(
        lambda *refs: down_kernel(len(xs), *refs),
        out_shape=jax.ShapeDtypeStruct((rows, rank2), jnp.bfloat16),
        grid=(adapters // 2,),
        in_specs=[pl.BlockSpec(memory_space=pltpu.SMEM), pl.BlockSpec((rows, 1), fixed)]
        + [pl.BlockSpec(x.shape, fixed) for x in xs]
        + [pl.BlockSpec((2, width, rank2), lambda a: (a, 0, 0))],
        out_specs=pl.BlockSpec((rows, rank2), fixed),
        scratch_shapes=[pltpu.VMEM((rows, rank2), jnp.float32)],
        compiler_params=pltpu.CompilerParams(vmem_limit_bytes=VMEM),
        cost_estimate=SMALL,
        name="down",
    )(ranks, ids, *xs, weight)


def up_kernel(count, id_ref, *refs):
    parts, weight_ref, outs = refs[:count], refs[count], refs[count + 1 :]
    adapters, halves, rank, columns = weight_ref.shape
    for out, (low, high) in zip(outs, spans([out.shape[0] for out in outs])):
        terms = [p[low:high] if len(p.shape) == 2 else p[n, low:high] for p in parts for n in range(p.shape[0] if len(p.shape) == 3 else 1)]
        total = terms[0].astype(jnp.float32)
        for term in terms[1:]:
            total = total + term.astype(jnp.float32)
        own = id_ref[low:high]
        for half in range(halves):
            shrink = total[:, half * rank : (half + 1) * rank]
            spread = jnp.concatenate(
                [jnp.where(own == a, shrink, 0.0).astype(jnp.bfloat16) for a in range(adapters)],
                axis=1,
            )
            matrix = weight_ref[:, half].reshape(adapters * rank, columns)
            out[:, half * columns : (half + 1) * columns] = jnp.dot(
                spread, matrix, preferred_element_type=jnp.float32
            ).astype(out.dtype)


def up(parts, ids, sizes, weight):
    _, halves, _, columns = weight.shape
    whole = pl.BlockSpec(memory_space=pltpu.VMEM)
    return pl.pallas_call(
        lambda *refs: up_kernel(len(parts), *refs),
        out_shape=[jax.ShapeDtypeStruct((n, halves * columns), jnp.bfloat16) for n in sizes],
        in_specs=[whole] * (2 + len(parts)),
        out_specs=[whole] * len(sizes),
        compiler_params=pltpu.CompilerParams(vmem_limit_bytes=VMEM),
        cost_estimate=SMALL,
        name="up",
    )(ids, *parts, weight)


def base_kernel(order_ref, x_ref, weight_ref, *outs):
    part = jnp.dot(x_ref[...], weight_ref[...], preferred_element_type=jnp.float32)
    if len(outs) == 1:
        outs[0][0] = part.astype(outs[0].dtype)
    else:
        share = pl.num_programs(0) // len(outs)
        for n, out in enumerate(outs):

            @pl.when(pl.program_id(0) // share == n)
            def _():
                out[0] = part.astype(out.dtype)


def base_blocks(x, weight, order, outputs, halves, columns, piece=0, pieces=1):
    rows, width = x.shape[0] // pieces, x.shape[1]
    blocks = order.shape[0]
    share = blocks // outputs

    def place(n):
        return lambda b, k, o: (
            jnp.clip(b - n * share, 0, share - 1),
            0,
            jnp.where(b < n * share, 0, jnp.where(b >= (n + 1) * share, halves - 1, k)),
        )

    return pl.pallas_call(
        base_kernel,
        out_shape=[jax.ShapeDtypeStruct((share, rows, halves * columns), jnp.bfloat16)] * outputs,
        grid_spec=pltpu.PrefetchScalarGridSpec(
            num_scalar_prefetch=1,
            grid=(blocks, halves),
            in_specs=[
                pl.BlockSpec((rows, width), lambda b, k, o: (piece, 0)),
                pl.BlockSpec((width, columns), lambda b, k, o: (0, k * blocks + o[b])),
            ],
            out_specs=[pl.BlockSpec((1, rows, columns), place(n)) for n in range(outputs)],
        ),
        compiler_params=pltpu.CompilerParams(vmem_limit_bytes=VMEM),
        cost_estimate=SMALL,
        name="base",
    )(order, x, weight)


def finish_kernel(starts, total_ref, target_ref, *refs):
    target, out_ref = target_ref[...], refs[-1]
    total = total_ref[...]
    for start, list_ref in zip(starts, refs):
        slot = start + lax.broadcasted_iota(jnp.int32, (1, list_ref.shape[0]), 1)
        sel = jnp.where(target == slot, 1.0, 0.0).astype(jnp.bfloat16)
        total = total + jnp.dot(sel, list_ref[...], preferred_element_type=jnp.float32)
    out_ref[...] = total.astype(out_ref.dtype)


def finish(total, target, starts, lists):
    rows, columns = total.shape
    tile = rows // 4
    return pl.pallas_call(
        lambda *refs: finish_kernel(starts, *refs),
        out_shape=jax.ShapeDtypeStruct((rows, columns), jnp.bfloat16),
        grid=(rows // tile,),
        in_specs=[
            pl.BlockSpec((tile, columns), lambda r: (r, 0)),
            pl.BlockSpec((tile, 1), lambda r: (r, 0)),
        ]
        + [pl.BlockSpec(part.shape, lambda r: (0, 0)) for part in lists],
        out_specs=pl.BlockSpec((tile, columns), lambda r: (r, 0)),
        compiler_params=pltpu.CompilerParams(vmem_limit_bytes=VMEM),
        cost_estimate=SMALL,
        name="finish",
    )(total, target, *lists)


def swap(x, axis, distance):
    count = lax.axis_size(axis)
    return lax.ppermute(x, axis, [(i, i ^ distance) for i in range(count)])


def together(*values):
    return lax.optimization_barrier(values)


def local(tokens, key_value_weight, adapter_down_weight, adapter_up_weight, row_adapter_index, ranks):
    steps, step_rows, width = tokens.shape
    inst_count = lax.axis_size("inst")
    tp_count = lax.axis_size("tp")
    held, _, rank2 = adapter_down_weight.shape
    halves, columns = adapter_up_weight.shape[1], adapter_up_weight.shape[3]
    rows = steps * step_rows
    me = lax.axis_index("inst")
    tp_me = lax.axis_index("tp")
    x = tokens.reshape(rows, width)
    ids = row_adapter_index.reshape(1, rows)
    chunk = 64
    pooled = inst_count == 4
    if pooled:
        own_cap, near_cap, far_cap, flex_cap = rows // 2, rows // 2, 224 * rows // 1024, 288 * rows // 1024
    else:
        own_cap = near_cap = far_cap = flex_cap = 0
    holder = ids // held
    base_near = own_cap
    base_far2 = base_near + near_cap
    base_flex = base_far2 + far_cap
    base_far3 = base_flex + flex_cap
    base_over = base_far3 + far_cap
    if pooled:
        cls = holder ^ me
        hit = (cls == jnp.arange(4)[:, None]).astype(jnp.bfloat16)
        earlier = (jnp.arange(rows)[:, None] < jnp.arange(rows)[None, :]).astype(jnp.bfloat16)
        before = jnp.dot(hit, earlier, preferred_element_type=jnp.float32).astype(jnp.int32)
        counts = jnp.sum(hit.astype(jnp.int32), axis=1)
        place = jnp.sum(jnp.where(hit > 0, before, 0), axis=0, keepdims=True)
        over_near = jnp.maximum(counts[1] - near_cap, 0)
        extra2 = jnp.maximum(counts[2] - far_cap, 0)
        extra3 = jnp.maximum(counts[3] - far_cap, 0)
        over_far = jnp.maximum(extra2 + extra3 - flex_cap, 0)
        flex = place - far_cap + jnp.where(cls == 3, extra2, 0)
        far_target = jnp.where(
            place < far_cap,
            place + jnp.where(cls == 2, base_far2, base_far3),
            jnp.where(flex < flex_cap, flex + base_flex, flex - flex_cap + over_near + base_over),
        )
        near_target = jnp.where(
            place < near_cap, place + base_near, place - near_cap + base_over
        )
        target = jnp.where(cls == 0, place, jnp.where(cls == 1, near_target, far_target))
        over = over_near + over_far
    else:
        target = jnp.arange(rows)[None, :]
        over = jnp.int32(rows)
    target_column = target.reshape(rows, 1)
    ids_column = ids.reshape(rows, 1)

    def slot_ids(start, size):
        sel = target_column == (start + jnp.arange(size))[None, :]
        return jnp.sum(jnp.where(sel, ids_column + 1, 0), axis=0, keepdims=True) - 1

    def put(start, rows_back):
        sel = target_column == (start + jnp.arange(rows_back.shape[0]))[None, :]
        return jnp.dot(
            sel.astype(jnp.bfloat16), rows_back, preferred_element_type=jnp.float32
        )

    def held_ids(global_ids):
        local_ids = global_ids.reshape(-1, 1) - me * held
        return jnp.where((local_ids >= 0) & (local_ids < held), local_ids, -1)

    def add(a, b):
        return (a.astype(jnp.float32) + b.astype(jnp.float32)).astype(jnp.bfloat16)

    def gathered(part):
        return lax.all_gather(part, "tp", axis=0, tiled=False)

    def exchange(part):
        if tp_count != 4:
            return [lax.psum(part.astype(jnp.float32), "tp")]
        pair = add(part, swap(part, "tp", 1))
        return [pair, swap(pair, "tp", 2)]

    def shrink(xs, list_ids):
        return down(xs, list_ids, adapter_down_weight, ranks)

    def expand(parts, list_ids, sizes):
        return up(parts, list_ids, sizes, adapter_up_weight)

    def base_parts(x):
        order = jnp.arange(tp_count, dtype=jnp.int32)
        (part,) = base_blocks(x, key_value_weight, order, 1, halves, columns)
        return part

    def base_sent(part):
        return lax.all_to_all(part, "tp", 0, 0, tiled=True)

    def largest(value, axis):
        count = lax.axis_size(axis)
        most = value
        for d in range(1, count):
            most = jnp.maximum(
                most, lax.ppermute(value, axis, [(i, (i + d) % count) for i in range(count)])
            )
        return most

    def add_overflow(total, trips):
        def more(carry):
            return carry[0] < trips

        def one(carry):
            trip, total = carry
            start = base_over + trip * chunk
            (mine,) = gather([0], [chunk], target - start, x)
            x_all = lax.all_gather(mine, "inst", axis=0, tiled=True)
            ids_all = held_ids(lax.all_gather(slot_ids(start, chunk), "inst", axis=0, tiled=True))
            part = exchange(shrink([x_all], ids_all))
            (delta,) = expand(part, ids_all, [inst_count * chunk])
            back = lax.all_to_all(
                delta.reshape(inst_count, chunk, halves * columns), "inst", 0, 0, tiled=True
            )
            mine = jnp.sum(back.astype(jnp.float32), axis=0).astype(jnp.bfloat16)
            return trip + 1, total + put(start, mine)

        return lax.while_loop(more, one, (jnp.int32(0), total))[1]

    if not pooled:
        trips = (largest(largest(over, "inst"), "groups") + chunk - 1) // chunk
        total = add_overflow(
            jnp.sum(base_sent(base_parts(x)).astype(jnp.float32), axis=0), trips
        )
        return total.astype(jnp.bfloat16).reshape(steps, step_rows, halves, columns)

    all_ids = slot_ids(0, base_over)
    over = jnp.full((1, 1), over, jnp.int32)
    got1 = swap(jnp.concatenate([all_ids[:, base_near:base_far2], over], axis=1), "inst", 1)
    got2 = swap(jnp.concatenate([all_ids[:, base_far2:base_far3], over], axis=1), "inst", 2)
    got3 = swap(jnp.concatenate([all_ids[:, base_flex:base_over], over], axis=1), "inst", 3)

    target, got1, got2, got3 = together(target, got1, got2, got3)
    (g_flex,) = gather([base_flex], [flex_cap], target, x)
    r_flex = swap(g_flex, "inst", 2)
    x, target, _ = together(x, target, g_flex)
    near = near_cap // 2
    (g_na,) = gather([base_near], [near], target, x)
    r_na = swap(g_na, "inst", 1)
    most = jnp.max(jnp.concatenate([over] + [g[:, -1:] for g in (got1, got2, got3)], axis=1))
    trips = (largest(most, "groups") + chunk - 1) // chunk
    k_1, k_2, k_3 = held_ids(got1[:, :-1]), held_ids(got2[:, :-1]), held_ids(got3[:, :-1])
    k_2, k_flex = k_2[:far_cap], k_2[far_cap:]
    k_on, k_3 = k_3[:flex_cap], k_3[flex_cap:]
    k_own = held_ids(all_ids[:, :own_cap])
    k_na, k_nb = k_1[:near_cap // 2], k_1[near_cap // 2 :]
    k_3_na = jnp.concatenate([k_3, k_na], axis=0)
    k_2_nb = jnp.concatenate([k_2, k_nb], axis=0)

    x, target, _ = together(x, target, g_na)
    g_3, g_own, g_2, g_nb = gather(
        [base_far3, 0, base_far2, base_near + near], [far_cap, own_cap, far_cap, near], target, x
    )
    x, g_own = together(x, g_own)
    part = base_parts(x)
    sent = base_sent(part)

    r_flex, r_na, g_3, g_2, g_nb, trips, k_flex, k_own, k_on, k_3_na, k_2_nb, _ = together(
        r_flex, r_na, g_3, g_2, g_nb, trips, k_flex, k_own, k_on, k_3_na, k_2_nb, part
    )
    r_3 = swap(g_3, "inst", 3)
    r_on = swap(r_flex, "inst", 1)
    s_flex = shrink([r_flex], k_flex)
    g_own, s_flex = together(g_own, s_flex)
    s_own = shrink([g_own], k_own)
    s_flex, s_own = together(s_flex, s_own)
    (d_flex,) = expand([gathered(s_flex)], k_flex, [flex_cap])

    r_3, r_na, g_2, g_nb, s_own, d_flex = together(r_3, r_na, g_2, g_nb, s_own, d_flex)
    r_2 = swap(g_2, "inst", 2)
    r_nb = swap(g_nb, "inst", 1)
    s_3_na = shrink([r_3, r_na], k_3_na)
    d_3, d_na = expand([gathered(s_3_na)], k_3_na, [far_cap, near])

    r_on, d_3, d_na = together(r_on, d_3, d_na)
    b_3, b_na = swap(d_3, "inst", 3), swap(d_na, "inst", 1)
    (d_on,) = expand([gathered(shrink([r_on], k_on))], k_on, [flex_cap])
    b_on = swap(d_on, "inst", 1)

    r_2, r_nb, d_on = together(r_2, r_nb, d_on)
    s_2_nb = shrink([r_2, r_nb], k_2_nb)
    s_2_nb, b_on = together(s_2_nb, b_on)
    back_flex = d_flex + b_on
    b_flex = swap(back_flex, "inst", 2)
    s_2_nb, _ = together(s_2_nb, back_flex)
    d_2, d_nb = expand([gathered(s_2_nb)], k_2_nb, [far_cap, near])
    d_2, d_nb, b_flex, b_3, b_na, e_own = together(d_2, d_nb, b_flex, b_3, b_na, gathered(s_own))
    b_2, b_nb = swap(d_2, "inst", 2), swap(d_nb, "inst", 1)
    e_own, sent, b_3, b_na, _ = together(e_own, sent, b_3, b_na, d_2)
    (d_own,) = expand([e_own], k_own, [own_cap])
    base = jnp.sum(sent.astype(jnp.float32), axis=0)
    total = add_overflow(base + put(0, jnp.concatenate([d_own, b_na], axis=0)), trips)
    total = total + put(base_far3, b_3)
    total = finish(
        total, target_column, [base_far2, base_flex, base_near + near], [b_2, b_flex, b_nb]
    )
    return total.reshape(steps, step_rows, halves, columns)


def solution(mesh):
    placed = (
        P(None, ("groups", "inst"), "tp"),
        P("tp", None),
        P(("groups", "inst"), "tp", None),
        P(("groups", "inst"), None, None, "tp"),
        P(None, ("groups", "inst")),
        P(("groups", "inst")),
    )
    return jax.shard_map(
        local,
        mesh=mesh,
        in_specs=placed,
        out_specs=P(None, ("groups", "inst"), None, "tp"),
        check_vma=False,
    )
```
